512 devices in a mesh: dp: 32 (over y, x, core), fsdp: 16 (over z).
Axes of the slice: x: 4, y: 4, z: 16, core: 2. Of those that a mesh axis runs over, the one named last changes fastest.
Arguments:
- patches: bfloat16 [1536, 1280, 128], P('dp', 'fsdp'), as said below
- patch_count: int32 [32, 48], P('dp'), may hold values from 0 to 128, as said below
- dest_rank: int32 [32, 48], P('dp'), may hold values from 0 to 31, as said below
- dest_slot: int32 [32, 48], P('dp'), may hold values from 0 to 23, as said below
- ln_gain: float32 [1280], replicated, may hold values from 0.5 to 1.5
- ln_bias: float32 [1280], replicated, may hold values from -3 to 3
- w_qkv: bfloat16 [3840, 1280], P('fsdp'), may hold values from -0.15625 to 0.15625
- b_qkv: bfloat16 [3840], P('fsdp'), may hold values from -3 to 3
Outputs:
- work_out: bfloat16 [768, 1280, 128], P('dp', 'fsdp')
The draws below stay inside these ranges and needn't reach their ends.
Inputs may be any that keep to these rules, and one draw needn't show every extreme that they name: `patches`: rows beyond a block's patch count hold arbitrary values. `patch_count`: the nonempty blocks of all ranks number 32 * 24 in all. `dest_rank`: read only where patch_count > 0: each nonempty block goes to its home rank or to the rank whose index differs by 32 / 2 (modulo 32); every rank receives exactly 24 nonempty blocks, and a rank sends at most 24 blocks away. `dest_slot`: read only where patch_count > 0: the nonempty blocks that one rank receives have distinct slots.
All inputs are finite; a program needn't handle non-finite values.
Results may differ from the reference program's by a relative error of at most 0.0059.
Values may be sent and summed in bfloat16 or wider, within the bound.
No kernel may reach another device: no remote copies, remote signals or barrier semaphores. Data moves between devices by JAX's collectives and lax.ppermute only.
A program may use at most 64 MiB of HBM per device.

```python
import math
import jax
import jax.numpy as jnp
from jax import lax

HEADS = 16
HEAD_DIM = 80
D = 1280
BLOCK = 128
HB = 48
WB = 24
N_DP = 32


def plan_tables(base_key):
    key_list = jax.random.split(base_key, 7)
    half_ranks = N_DP // 2
    flips = jax.random.randint(key_list[0], (half_ranks,), 0, 2)
    shifts = jax.random.randint(key_list[1], (half_ranks,), (WB + 1) // 2, WB + 1).at[0].set(WB)
    lower_loads = WB + jnp.where(flips == 1, shifts, -shifts)
    block_loads = jnp.concatenate([lower_loads, 2 * WB - lower_loads]).astype(jnp.int32)
    rank_ids = jnp.arange(N_DP, dtype=jnp.int32)
    partner = (rank_ids + half_ranks) % N_DP

    def shuffle_home(row_key):
        return jax.random.permutation(row_key, HB)

    def shuffle_work(row_key):
        return jax.random.permutation(row_key, WB)
    orders = jax.vmap(shuffle_home)(jax.random.split(key_list[2], N_DP)).astype(jnp.int32)
    slot_perm = jax.vmap(shuffle_work)(jax.random.split(key_list[3], N_DP)).astype(jnp.int32)
    occupied = orders < block_loads[:, None]
    kept = orders < jnp.minimum(block_loads, WB)[:, None]
    partner_load = block_loads[partner]
    moved_index = jnp.clip(partner_load[:, None] + orders - WB, 0, WB - 1)
    own_slot = jnp.take_along_axis(slot_perm, jnp.clip(orders, 0, WB - 1), axis=1)
    partner_slot = jnp.take_along_axis(slot_perm[partner], moved_index, axis=1)
    filler_rank = jax.random.randint(key_list[4], (N_DP, HB), 0, N_DP)
    filler_slot = jax.random.randint(key_list[5], (N_DP, HB), 0, WB)
    ranks_out = jnp.where(kept, rank_ids[:, None], jnp.where(occupied, partner[:, None], filler_rank))
    slots_out = jnp.where(kept, own_slot, jnp.where(occupied, partner_slot, filler_slot))
    counts = jnp.where(occupied, jax.random.randint(key_list[6], (N_DP, HB), 1, BLOCK + 1), 0)
    busy_rank = jnp.where(flips[0] == 1, 0, half_ranks)
    full_spot = (rank_ids[:, None] == busy_rank) & (orders == 0)
    counts = jnp.where(full_spot, BLOCK, counts)
    return (counts.astype(jnp.int32), ranks_out.astype(jnp.int32), slots_out.astype(jnp.int32))


def draw_patch_count(key, part):
    tables = plan_tables(key)
    return tables[0]


def draw_dest_rank(key, part):
    tables = plan_tables(key)
    return tables[1]


def draw_dest_slot(key, part):
    tables = plan_tables(key)
    return tables[2]


def draw_patches(key, part):
    key = jax.random.fold_in(key, 11)
    key_list = jax.random.split(key, 3)
    full_shape = (N_DP * HB, D, BLOCK)
    feature_index = jnp.arange(D, dtype=jnp.float32) / D
    col_scale = jnp.exp(jax.random.uniform(key_list[1], (D,), minval=0.0, maxval=math.log(10.0)))
    row_scale = jnp.exp(jax.random.uniform(key_list[2], (N_DP * HB, 1, BLOCK), minval=0.0, maxval=math.log(10.0)))
    rising = jnp.exp(math.log(3.0) * feature_index)
    noise = jax.random.truncated_normal(key_list[0], -5.0, 5.0, full_shape)
    return (noise * (col_scale * rising)[:, None] * row_scale).astype(jnp.bfloat16)


def steps_of(rng, shape, shards, low, top_value):
    loudness, own = 1.0, jax.random.fold_in(rng, 6)
    for position, parts in shards:
        heights = jnp.exp(jax.random.uniform(jax.random.fold_in(own, position), (parts,), jnp.float32, low / len(shards), top_value / len(shards)))
        loudness = loudness * jnp.repeat(heights, shape[position] // parts).reshape([-1 if axis == position else 1 for axis in range(len(shape))])
    return loudness


def bell_draw(own_key, extent, deviation, most, cuts=(), kind=jnp.bfloat16):
    result = deviation * jax.random.normal(own_key, extent, jnp.float32)
    if cuts:
        result = result * steps_of(own_key, extent, cuts, -0.22, 0.18)
    return jnp.clip(result, -most, most).astype(kind)


def setup_inputs(seed: int = 0) -> dict:
    key_of = jax.random.split(jax.random.key(seed), 9)
    patches = draw_patches(jax.random.fold_in(key_of[8], 71), 0)
    patch_count = draw_patch_count(jax.random.fold_in(key_of[8], 71), 0)
    dest_rank = draw_dest_rank(jax.random.fold_in(key_of[8], 71), 0)
    dest_slot = draw_dest_slot(jax.random.fold_in(key_of[8], 71), 0)
    ln_gain = jnp.clip(jax.random.uniform(key_of[4], (D,), jnp.float32, 0.5, 1.5), 0.5, 1.5)
    ln_bias = bell_draw(key_of[5], (D,), 0.5, 3.0, (), jnp.float32)
    w_qkv = bell_draw(key_of[6], (3 * D, D), D ** -0.5, 0.15625, ((0, 16),))
    b_qkv = bell_draw(key_of[7], (3 * D,), 0.5, 3.0, ((0, 16),))
    return {"patches": patches, "patch_count": patch_count, "dest_rank": dest_rank, "dest_slot": dest_slot, "ln_gain": ln_gain, "ln_bias": ln_bias, "w_qkv": w_qkv, "b_qkv": b_qkv}


def layer_norm(blocks, scale_vec, offset_vec):
    values = blocks.astype(jnp.float32)
    center = lax.optimization_barrier(jnp.mean(values, axis=1, keepdims=True))
    spread = lax.optimization_barrier(jnp.mean(jnp.square(values - center), axis=1, keepdims=True))
    return ((values - center) * lax.rsqrt(spread + 1e-06) * scale_vec[:, None] + offset_vec[:, None]).astype(jnp.bfloat16)

def attend(qkv_rows, counts, head_total):
    blocks_n, block_rows, _ = qkv_rows.shape
    divided = qkv_rows.reshape(blocks_n, block_rows, head_total, 3, HEAD_DIM).astype(jnp.float32)
    query_part = divided[:, :, :, 0]
    key_part = divided[:, :, :, 1]
    value_part = divided[:, :, :, 2]
    scores = jnp.einsum('bqhd,bkhd->bhqk', query_part, key_part) / math.sqrt(HEAD_DIM)
    places = jnp.arange(block_rows, dtype=jnp.int32)
    inside = (places[None, :] < counts[:, None]).astype(scores.dtype)
    raised = jnp.exp(scores) * inside[:, None, None, :]
    totals = lax.optimization_barrier(jnp.sum(raised, axis=-1, keepdims=True))
    totals = jnp.where(counts[:, None, None, None] > 0, totals, 1.0)
    weights = (raised / totals).astype(jnp.bfloat16)
    mixed = jnp.einsum('bhqk,bkhd->bhdq', weights.astype(jnp.float32), value_part)
    mixed = mixed * inside[:, None, None, :]
    return mixed.reshape(blocks_n, head_total * HEAD_DIM, block_rows).astype(jnp.bfloat16)

def reference(patches, patch_count, dest_rank, dest_slot, ln_gain, ln_bias, w_qkv, b_qkv):
    occupied = patch_count > 0
    target = jnp.where(occupied, dest_rank * WB + dest_slot, N_DP * WB).reshape(-1).astype(jnp.int32)
    holder = jnp.zeros((N_DP * WB + 1, D, BLOCK), jnp.bfloat16).at[target].set(patches)
    work_rows = holder[:N_DP * WB]
    work_counts = jnp.zeros((N_DP * WB + 1,), jnp.int32).at[target].set(patch_count.reshape(-1).astype(jnp.int32))
    work_counts = work_counts[:N_DP * WB]

    def encode_rank(inputs):
        blocks, counts = inputs
        normed = layer_norm(blocks, ln_gain, ln_bias)
        projected = jnp.einsum('bfr,cf->brc', normed.astype(jnp.float32), w_qkv.astype(jnp.float32))
        qkv_rows = (projected + b_qkv.astype(jnp.float32)).astype(jnp.bfloat16)
        return attend(qkv_rows, counts, HEADS)
    encoded = lax.map(encode_rank, (work_rows.reshape(N_DP, WB, D, BLOCK), work_counts.reshape(N_DP, WB)))
    return encoded.reshape(N_DP * WB, D, BLOCK)
```

```python
import math

import jax
import jax.numpy as jnp
from jax import lax
from jax.sharding import PartitionSpec as P

HEAD_DIM = 80


def passed_along(value, axis, steps):
    count = lax.axis_size(axis)
    pairs = [(source, (source + steps) % count) for source in range(count)]
    return lax.ppermute(value, axis, pairs)


def attend(qkv_rows, counts, head_total):
    blocks_n, block_rows, _ = qkv_rows.shape
    divided = qkv_rows.reshape(blocks_n, block_rows, head_total, 3, HEAD_DIM)
    query_part = divided[:, :, :, 0]
    key_part = divided[:, :, :, 1]
    value_part = divided[:, :, :, 2]
    scores = jnp.einsum(
        "bqhd,bkhd->bhqk", query_part, key_part, preferred_element_type=jnp.float32
    ) / math.sqrt(HEAD_DIM)
    places = jnp.arange(block_rows, dtype=jnp.int32)
    inside = (places[None, :] < counts[:, None]).astype(jnp.float32)
    raised = jnp.exp(scores) * inside[:, None, None, :]
    totals = jnp.sum(raised, axis=-1, keepdims=True)
    totals = jnp.where(counts[:, None, None, None] > 0, totals, 1.0)
    weights = (raised / totals).astype(jnp.bfloat16)
    mixed = jnp.einsum("bhqk,bkhd->bhdq", weights, value_part, preferred_element_type=jnp.float32)
    mixed = mixed * inside[:, None, None, :]
    return mixed.reshape(blocks_n, head_total * HEAD_DIM, block_rows).astype(jnp.bfloat16)


def encode(blocks, counts, ln_gain, ln_bias, w_qkv, b_qkv):
    head_local = w_qkv.shape[0] // (3 * HEAD_DIM)
    gathered = lax.all_gather(blocks, "fsdp", axis=1, tiled=True)
    values = gathered.astype(jnp.float32)
    feat_total = values.shape[1]
    center = jnp.sum(values, axis=1) / feat_total
    spread = jnp.sum(values * values, axis=1) / feat_total - center * center
    scaled = (values - center[:, None, :]) * lax.rsqrt(spread + 1e-06)[:, None, :]
    normed = (scaled * ln_gain[:, None] + ln_bias[:, None]).astype(jnp.bfloat16)
    projected = jnp.einsum(
        "bfr,cf->brc",
        normed,
        w_qkv,
        preferred_element_type=jnp.float32,
    )
    qkv_rows = (projected + b_qkv.astype(jnp.float32)).astype(jnp.bfloat16)
    return attend(qkv_rows, counts, head_local)


def shards(patches, patch_count, dest_rank, dest_slot, ln_gain, ln_bias, w_qkv, b_qkv):
    rank_total = lax.axis_size("dp")
    own_rank = lax.axis_index("dp")
    home_blocks, feat_share, block_rows = patches.shape
    work_blocks = home_blocks // 2
    counts = patch_count[0]
    dest_ranks = dest_rank[0]
    dest_slots = dest_slot[0]
    occupied = counts > 0
    staying = occupied & (dest_ranks == own_rank)
    leaving = occupied & (dest_ranks != own_rank)
    positions = jnp.arange(home_blocks, dtype=jnp.int32)
    earlier = leaving[None, :] & (positions[None, :] < positions[:, None])
    leave_order = jnp.sum(earlier.astype(jnp.int32), axis=1)
    target = jnp.where(leaving, leave_order, work_blocks)
    matches = target[None, :] == jnp.arange(work_blocks, dtype=jnp.int32)[:, None]
    filled = jnp.any(matches, axis=1)
    chosen = jnp.sum(jnp.where(matches, positions[None, :], 0), axis=1)
    label_pack = jnp.stack(
        (jnp.where(filled, counts[chosen], 0), jnp.where(filled, dest_slots[chosen], 0)), axis=-1
    )
    label_pack = label_pack.astype(jnp.bfloat16)
    arrived, arrived_labels = passed_along(
        (patches[chosen] * filled[:, None, None].astype(patches.dtype), label_pack),
        "dp",
        rank_total // 2,
    )
    pool = jnp.concatenate([patches, arrived], axis=0)
    pool_counts = jnp.concatenate(
        [jnp.where(staying, counts, 0), arrived_labels[:, 0].astype(jnp.int32)]
    )
    pool_slots = jnp.concatenate([dest_slots, arrived_labels[:, 1].astype(jnp.int32)])
    pool_size = pool.shape[0]
    landing = (pool_slots[None, :] == jnp.arange(work_blocks, dtype=jnp.int32)[:, None]) & (
        pool_counts[None, :] > 0
    )
    present = jnp.any(landing, axis=1)
    source_index = jnp.sum(
        jnp.where(landing, jnp.arange(pool_size, dtype=jnp.int32)[None, :], 0), axis=1
    )
    work_rows = pool[source_index] * present[:, None, None].astype(pool.dtype)
    work_counts = jnp.sum(jnp.where(landing, pool_counts[None, :], 0), axis=1)
    work_rows, work_counts = (work_rows, work_counts)
    return encode(work_rows, work_counts, ln_gain, ln_bias, w_qkv, b_qkv)


def solution(mesh):
    placed = (
        P("dp", "fsdp", None),
        P("dp", None),
        P("dp", None),
        P("dp", None),
        P(),
        P(),
        P("fsdp", None),
        P("fsdp"),
    )
    return jax.shard_map(
        shards, mesh=mesh, in_specs=placed, out_specs=P("dp", "fsdp", None), check_vma=False
    )
```

```python
import math

import jax
import jax.numpy as jnp
from jax import lax
from jax.experimental import pallas as pl
from jax.experimental.pallas import tpu as pltpu
from jax.sharding import PartitionSpec as P

HEAD_DIM = 80
GROUP = 4


def encode_kernel(starts, counts, weight, column_sum, shift, *refs):
    pieces, out, rows, qkv = refs[:-3], refs[-3], refs[-2], refs[-1]
    feat_share, block_rows = out.shape[1], out.shape[2]
    columns_n = qkv.shape[0]
    feat_total = feat_share * len(pieces)
    step = pl.program_id(0)
    squares = []
    for block in range(GROUP):
        columns = slice(block * block_rows, (block + 1) * block_rows)
        sum_two = jnp.zeros((feat_share, block_rows), jnp.float32)
        for index, piece in enumerate(pieces):
            raw = piece[block]
            rows[pl.ds(pl.multiple_of(starts[index], 16), feat_share), columns] = raw
            values = raw.astype(jnp.float32)
            sum_two += values * values
        squares.append(jnp.sum(sum_two, axis=0, keepdims=True))
    product = jnp.dot(weight[...], rows[...], preferred_element_type=jnp.float32)
    center = product[columns_n : columns_n + 1] / feat_total
    spread = jnp.concatenate(squares, axis=1) / feat_total - center * center
    scale = lax.rsqrt(spread + 1e-06)
    projected = (product[:columns_n] - column_sum[...] * center) * scale + shift[...]
    qkv[...] = projected.astype(jnp.bfloat16)
    key_place = lax.broadcasted_iota(jnp.int32, (block_rows, block_rows), 0)
    row_place = lax.broadcasted_iota(jnp.int32, (feat_share, block_rows), 1)
    for block in range(GROUP):
        count = counts[step * GROUP + block]
        columns = slice(block * block_rows, (block + 1) * block_rows)
        query_part = qkv[0:HEAD_DIM, columns]
        key_part = qkv[HEAD_DIM : 2 * HEAD_DIM, columns]
        value_part = qkv[2 * HEAD_DIM : 3 * HEAD_DIM, columns]
        scores = lax.dot_general(
            key_part, query_part, (((0,), (0,)), ((), ())), preferred_element_type=jnp.float32
        ) * (1.0 / math.sqrt(HEAD_DIM))
        raised = jnp.where(key_place < count, jnp.exp(scores), 0.0)
        totals = jnp.sum(raised, axis=0, keepdims=True)
        totals = jnp.where(count > 0, totals, 1.0)
        weights = (raised * (1.0 / totals)).astype(jnp.bfloat16)
        mixed = jnp.dot(value_part, weights, preferred_element_type=jnp.float32)
        out[block] = jnp.where(row_place < count, mixed, 0.0).astype(jnp.bfloat16)


def folded(ln_gain, ln_bias, w_qkv, b_qkv):
    wide = w_qkv.astype(jnp.float32)
    scaled = (wide * ln_gain[None, :]).astype(jnp.bfloat16)
    column_sum = jnp.sum(scaled.astype(jnp.float32), axis=1, keepdims=True)
    shift = jnp.sum(wide * ln_bias[None, :], axis=1) + b_qkv.astype(jnp.float32)
    ones = jnp.ones((16, w_qkv.shape[1]), jnp.bfloat16)
    return jnp.concatenate([scaled, ones], axis=0), column_sum, shift[:, None]


def encode(pieces, starts, counts, weight, column_sum, shift):
    blocks_n, feat_share, block_rows = pieces[0].shape
    feat_total = feat_share * len(pieces)
    columns_n = column_sum.shape[0]

    def whole(step, starts_ref, counts_ref):
        return (0, 0)

    def group(step, starts_ref, counts_ref):
        return (step, 0, 0)

    block_spec = pl.BlockSpec((GROUP, feat_share, block_rows), group)
    return pl.pallas_call(
        encode_kernel,
        grid_spec=pltpu.PrefetchScalarGridSpec(
            num_scalar_prefetch=2,
            grid=(blocks_n // GROUP,),
            in_specs=[
                pl.BlockSpec(weight.shape, whole),
                pl.BlockSpec((columns_n, 1), whole),
                pl.BlockSpec((columns_n, 1), whole),
            ]
            + [block_spec] * len(pieces),
            out_specs=block_spec,
            scratch_shapes=[
                pltpu.VMEM((feat_total, GROUP * block_rows), jnp.bfloat16),
                pltpu.VMEM((columns_n, GROUP * block_rows), jnp.bfloat16),
            ],
        ),
        out_shape=jax.ShapeDtypeStruct((blocks_n, feat_share, block_rows), jnp.bfloat16),
        compiler_params=pltpu.CompilerParams(vmem_limit_bytes=60 * 2**20),
        cost_estimate=pl.CostEstimate(
            flops=2 * blocks_n * block_rows * columns_n * feat_total,
            bytes_accessed=2 * feat_total * blocks_n * block_rows,
            transcendentals=blocks_n * block_rows * block_rows,
        ),
    )(starts, counts, weight, column_sum, shift, *pieces)


def rebalance(patches, counts, dest_ranks, dest_slots):
    rank_total = lax.axis_size("dp")
    own_rank = lax.axis_index("dp")
    home_blocks = patches.shape[0]
    work_blocks = home_blocks // 2
    occupied = counts > 0
    staying = occupied & (dest_ranks == own_rank)
    leaving = occupied & (dest_ranks != own_rank)
    positions = jnp.arange(home_blocks, dtype=jnp.int32)
    work_slots = jnp.arange(work_blocks, dtype=jnp.int32)
    earlier = leaving[None, :] & (positions[None, :] < positions[:, None])
    leave_order = jnp.sum(earlier.astype(jnp.int32), axis=1)
    target = jnp.where(leaving, leave_order, work_blocks)
    matches = target[None, :] == work_slots[:, None]

    def picked(values):
        return jnp.sum(jnp.where(matches, values[None, :], 0), axis=1)

    pairs = [(source, (source + rank_total // 2) % rank_total) for source in range(rank_total)]
    labels = jnp.stack((picked(counts), picked(dest_slots)), axis=0).astype(patches.dtype)
    label_block = jnp.zeros((1,) + patches.shape[1:], patches.dtype)
    label_block = lax.dynamic_update_slice(label_block, labels[None], (0, 0, 0))
    message = jnp.concatenate([patches[picked(positions)], label_block], axis=0)
    arrived = lax.ppermute(message, "dp", pairs)
    arrived_labels = arrived[work_blocks, :2, :work_blocks].astype(jnp.int32)
    arrived = arrived[:work_blocks]
    pool = jnp.concatenate([patches, arrived], axis=0)
    pool_counts = jnp.concatenate([jnp.where(staying, counts, 0), arrived_labels[0]])
    pool_slots = jnp.concatenate([dest_slots, arrived_labels[1]])
    landing = (pool_slots[None, :] == work_slots[:, None]) & (pool_counts[None, :] > 0)
    pool_places = jnp.arange(pool.shape[0], dtype=jnp.int32)
    source_index = jnp.sum(jnp.where(landing, pool_places[None, :], 0), axis=1)
    work_counts = jnp.sum(jnp.where(landing, pool_counts[None, :], 0), axis=1)
    return pool[source_index], work_counts


def gather_pieces(own):
    rank_total, ring = lax.axis_size("dp"), lax.axis_size("fsdp")
    swaps = [(rank, rank ^ 1) for rank in range(rank_total)]
    hops = [
        (rank * ring + place, rank * ring + (place + 1 - 2 * (rank % 2)) % ring)
        for rank in range(rank_total)
        for place in range(ring)
    ]

    def swap(value):
        return lax.ppermute(value, "dp", swaps)

    def hop(value):
        return lax.ppermute(value, ("dp", "fsdp"), hops)

    place = lax.axis_index("fsdp")
    sense = 1 - 2 * (lax.axis_index("dp") % 2)
    pieces, origins = [own], [place]
    mine, other = hop(own), swap(own)
    swaps_done = []
    for step in range(1, ring // 2 + 1):
        pieces.append(mine)
        origins.append((place - sense * step) % ring)
        if step < ring // 2:
            received = other = hop(other)
            if step > 2:
                other, swaps_done[step - 3] = lax.optimization_barrier((other, swaps_done[step - 3]))
            mine = hop(mine)
            swaps_done.append(swap(received))
            origins.append((place + sense * step) % ring)
    first, rest = pieces[0], pieces[1:]
    pieces = [first]
    for step in range(len(rest)):
        pieces.append(rest[step])
        if step < len(swaps_done):
            pieces.append(swaps_done[step])
    return pieces, jnp.stack(origins).astype(jnp.int32)


def shards(patches, patch_count, dest_rank, dest_slot, ln_gain, ln_bias, w_qkv, b_qkv):
    work_rows, work_counts = rebalance(patches, patch_count[0], dest_rank[0], dest_slot[0])
    weight, column_sum, shift = folded(ln_gain, ln_bias, w_qkv, b_qkv)
    work_rows, weight, column_sum, shift = lax.optimization_barrier(
        (work_rows, weight, column_sum, shift)
    )
    pieces, origins = gather_pieces(work_rows)
    starts = origins * patches.shape[1]
    return encode(pieces, starts, work_counts, weight, column_sum, shift)


def solution(mesh):
    placed = (
        P("dp", "fsdp", None),
        P("dp", None),
        P("dp", None),
        P("dp", None),
        P(),
        P(),
        P("fsdp", None),
        P("fsdp"),
    )
    return jax.shard_map(
        shards, mesh=mesh, in_specs=placed, out_specs=P("dp", "fsdp", None), check_vma=False
    )
```

```python
import math

import jax
import jax.numpy as jnp
from jax import lax
from jax.experimental import pallas as pl
from jax.experimental.pallas import tpu as pltpu
from jax.sharding import PartitionSpec as P

HEAD_DIM = 80
GROUP = 8
SUMS = 16


def encode_kernel(counts, weight, column_sum, shift, *refs):
    pieces, out = refs[:-1], refs[-1]
    blocks_n, feat_share, block_rows = out.shape
    columns_n = column_sum.shape[0]
    feat_total = feat_share * len(pieces)
    key_place = lax.broadcasted_iota(jnp.int32, (block_rows, block_rows), 0)
    row_place = lax.broadcasted_iota(jnp.int32, (feat_share, block_rows), 1)

    def encode_group(first):
        blocks, squares = [], []
        for block in range(GROUP):
            raw = jnp.concatenate([piece[first + block] for piece in pieces], axis=0)
            values = raw.astype(jnp.float32)
            square = jnp.sum((values * values).reshape(feat_total // 8, 8, block_rows), axis=0)
            squares.append(jnp.sum(square, axis=0, keepdims=True))
            blocks.append(raw)
        product = jnp.dot(
            weight[...], jnp.concatenate(blocks, axis=1), preferred_element_type=jnp.float32
        )
        center = product[columns_n : columns_n + 1] / feat_total
        spread = jnp.concatenate(squares, axis=1) / feat_total - center * center
        scale = lax.rsqrt(spread + 1e-06)
        for block in range(GROUP):
            columns = slice(block * block_rows, (block + 1) * block_rows)
            part = (product[:columns_n, columns] - column_sum[...] * center[:, columns]) * scale[:, columns]
            qkv = (part + shift[...]).astype(jnp.bfloat16)
            count = counts[first + block]
            scores = lax.dot_general(
                qkv[HEAD_DIM : 2 * HEAD_DIM],
                qkv[:HEAD_DIM],
                (((0,), (0,)), ((), ())),
                preferred_element_type=jnp.float32,
            ) * (1.0 / math.sqrt(HEAD_DIM))
            raised = jnp.where(key_place < count, jnp.exp(scores), 0.0)
            totals = jnp.sum(raised, axis=0, keepdims=True)
            totals = jnp.where(count > 0, totals, 1.0)
            weights = (raised * (1.0 / totals)).astype(jnp.bfloat16)
            mixed = jnp.dot(qkv[2 * HEAD_DIM :], weights, preferred_element_type=jnp.float32)
            out[first + block] = jnp.where(row_place < count, mixed, 0.0).astype(jnp.bfloat16)

    @pl.loop(0, blocks_n // GROUP)
    def _(index):
        encode_group(index * GROUP)


def folded(ln_gain, ln_bias, w_qkv, b_qkv, origins, block_rows):
    columns_n, feat_total = w_qkv.shape
    wide = w_qkv.astype(jnp.float32)
    scaled = (wide * ln_gain[None, :]).astype(jnp.bfloat16)
    column_sum = jnp.sum(scaled.astype(jnp.float32), axis=1, keepdims=True)
    shift = jnp.sum(wide * ln_bias[None, :], axis=1) + b_qkv.astype(jnp.float32)
    ones = jnp.ones((SUMS, feat_total), jnp.bfloat16)
    weight = jnp.concatenate([scaled, ones], axis=0)
    share = feat_total // len(origins)
    inside = jnp.arange(share, dtype=jnp.int32)
    order = (jnp.stack(origins)[:, None] * share + inside[None, :]).reshape(-1)
    places = jnp.arange(feat_total, dtype=jnp.int32)
    moved = (places[:, None] == order[None, :]).astype(jnp.bfloat16)
    weight = jnp.dot(weight, moved, preferred_element_type=jnp.bfloat16)
    column_sum = jnp.broadcast_to(column_sum, (columns_n, block_rows))
    shift = jnp.broadcast_to(shift[:, None], (columns_n, block_rows))
    return weight, column_sum, shift


def encode(pieces, counts, weight, column_sum, shift):
    blocks_n, feat_share, block_rows = pieces[0].shape
    feat_total = feat_share * len(pieces)
    rows_n = blocks_n * block_rows
    vmem = pl.BlockSpec(memory_space=pltpu.VMEM)
    return pl.pallas_call(
        encode_kernel,
        in_specs=[pl.BlockSpec(memory_space=pltpu.SMEM), vmem, vmem, vmem]
        + [vmem] * len(pieces),
        out_specs=vmem,
        out_shape=jax.ShapeDtypeStruct((blocks_n, feat_share, block_rows), jnp.bfloat16),
        compiler_params=pltpu.CompilerParams(vmem_limit_bytes=24 * 2**20),
        cost_estimate=pl.CostEstimate(
            flops=2 * rows_n * weight.shape[0] * feat_total,
            bytes_accessed=2 * feat_total * rows_n,
            transcendentals=blocks_n * block_rows * block_rows,
        ),
    )(counts, weight, column_sum, shift, *pieces)


def rebalance(patches, counts, dest_ranks, dest_slots, ready):
    rank_total = lax.axis_size("dp")
    home_blocks = patches.shape[0]
    work_blocks = home_blocks // 2
    staying = dest_ranks == lax.axis_index("dp")
    positions = jnp.arange(home_blocks, dtype=jnp.int32)
    work_slots = jnp.arange(work_blocks, dtype=jnp.int32)
    filling = (dest_slots[None, :] == work_slots[:, None]) & (counts[None, :] > 0)

    def picked(which, values):
        return jnp.sum(jnp.where(filling & which[None, :], values[None, :], 0), axis=1)

    leaving_counts = picked(~staying, counts)
    staying_counts = picked(staying, counts)
    label_block = jnp.zeros((1,) + patches.shape[1:], patches.dtype)
    label_block = lax.dynamic_update_slice(
        label_block, leaving_counts.astype(patches.dtype)[None, None], (0, 0, 0)
    )
    message = jnp.concatenate([patches[picked(~staying, positions)], label_block], axis=0)
    pairs = [(source, (source + rank_total // 2) % rank_total) for source in range(rank_total)]
    arrived = lax.ppermute(message, "dp", pairs)
    sources = jnp.where(staying_counts > 0, picked(staying, positions), home_blocks + work_slots)
    arrived, sources, ready = lax.optimization_barrier((arrived, sources, ready))
    arrived_counts = arrived[work_blocks, 0, :work_blocks].astype(jnp.int32)
    pool = jnp.concatenate([patches, arrived], axis=0)
    work_counts = jnp.where(staying_counts > 0, staying_counts, arrived_counts)
    return pool[sources], work_counts, ready


def gather_pieces(own):
    rank_total, ring = lax.axis_size("dp"), lax.axis_size("fsdp")
    swaps = [(rank, rank ^ 1) for rank in range(rank_total)]
    hops = [
        (rank * ring + place, rank * ring + (place + 1 - 2 * (rank % 2)) % ring)
        for rank in range(rank_total)
        for place in range(ring)
    ]

    def swap(value):
        return lax.ppermute(value, "dp", swaps)

    def hop(value):
        return lax.ppermute(value, ("dp", "fsdp"), hops)

    half = ring // 2
    mine, other, swapped = [own, hop(own)], [swap(own)], {}
    for step in range(1, half):
        received = hop(other[-1])
        other.append(received)
        mine[-1], other[-2] = lax.optimization_barrier((mine[-1], other[-2]))
        if step > 2:
            other[-1], swapped[step - 2] = lax.optimization_barrier((received, swapped[step - 2]))
        mine.append(hop(mine[-1]))
        swapped[step] = swap(received)

    pieces = [own]
    for step in range(1, half + 1):
        pieces.append(mine[step])
        if step < half:
            pieces.append(swapped[step])
    return pieces


def shards(patches, patch_count, dest_rank, dest_slot, ln_gain, ln_bias, w_qkv, b_qkv):
    ring = lax.axis_size("fsdp")
    place = lax.axis_index("fsdp")
    sense = 1 - 2 * (lax.axis_index("dp") % 2)
    origins = [place]
    for step in range(1, ring // 2 + 1):
        origins.append((place - sense * step) % ring)
        if step < ring // 2:
            origins.append((place + sense * step) % ring)
    weight, column_sum, shift = folded(
        ln_gain, ln_bias, w_qkv, b_qkv, origins, patches.shape[2]
    )
    own, counts, ready = rebalance(
        patches, patch_count[0], dest_rank[0], dest_slot[0], (weight, column_sum, shift)
    )
    return encode(gather_pieces(own), counts, *ready)


def solution(mesh):
    placed = (
        P("dp", "fsdp", None),
        P("dp", None),
        P("dp", None),
        P("dp", None),
        P(),
        P(),
        P("fsdp", None),
        P("fsdp"),
    )
    return jax.shard_map(
        shards, mesh=mesh, in_specs=placed, out_specs=P("dp", "fsdp", None), check_vma=False
    )
```

```python
import functools
import math

import jax
import jax.numpy as jnp
from jax import lax
from jax.experimental import pallas as pl
from jax.experimental.pallas import tpu as pltpu
from jax.sharding import PartitionSpec as P

HEAD_DIM = 80
GROUP = 12
SUMS = 16


def project_group(weight, pieces, first):
    _, feat_share, block_rows = pieces[0].shape
    feat_total = feat_share * len(pieces)
    blocks, squares = [], []
    for block in range(GROUP):
        raw = jnp.concatenate([piece[first + block] for piece in pieces], axis=0)
        values = raw.astype(jnp.float32)
        squares.append(jnp.sum((values * values).reshape(feat_total // 8, 8, block_rows), axis=0))
        blocks.append(raw)
    product = jnp.dot(
        weight[...], jnp.concatenate(blocks, axis=1), preferred_element_type=jnp.float32
    )
    return product[:-8], jnp.concatenate(squares, axis=1)


def project_kernel(weight, *refs):
    pieces, out = refs[:-1], refs[-1]

    @pl.loop(0, out.shape[0])
    def _(index):
        product, squares = project_group(weight, pieces, index * GROUP)
        out[index, :-8] = product
        out[index, -8:] = squares


def attend_kernel(feat_total, counts, weight, column_sum, shift, before, *refs):
    pieces, out = refs[:-1], refs[-1]
    blocks_n, feat_share, block_rows = out.shape
    columns_n = column_sum.shape[0]
    key_place = lax.broadcasted_iota(jnp.int32, (block_rows, block_rows), 0)
    row_place = lax.broadcasted_iota(jnp.int32, (feat_share, block_rows), 1)

    @pl.loop(0, blocks_n // GROUP)
    def _(index):
        first = index * GROUP
        product, squares = project_group(weight, pieces, first)
        product = product + before[index, :-8]
        squares = jnp.sum(squares + before[index, -8:], axis=0, keepdims=True)
        center = product[columns_n : columns_n + 1] / feat_total
        spread = squares / feat_total - center * center
        scale = lax.rsqrt(spread + 1e-06)
        for block in range(GROUP):
            columns = slice(block * block_rows, (block + 1) * block_rows)
            part = (product[:columns_n, columns] - column_sum[...] * center[:, columns]) * scale[:, columns]
            qkv = (part + shift[...]).astype(jnp.bfloat16)
            count = counts[first + block]
            scores = lax.dot_general(
                qkv[HEAD_DIM : 2 * HEAD_DIM],
                qkv[:HEAD_DIM],
                (((0,), (0,)), ((), ())),
                preferred_element_type=jnp.float32,
            ) * (1.0 / math.sqrt(HEAD_DIM))
            raised = jnp.where(key_place < count, jnp.exp(scores), 0.0)
            totals = jnp.sum(raised, axis=0, keepdims=True)
            totals = jnp.where(count > 0, totals, 1.0)
            weights = (raised * (1.0 / totals)).astype(jnp.bfloat16)
            mixed = jnp.dot(qkv[2 * HEAD_DIM :], weights, preferred_element_type=jnp.float32)
            out[first + block] = jnp.where(row_place < count, mixed, 0.0).astype(jnp.bfloat16)


def folded(ln_gain, ln_bias, w_qkv, b_qkv, origins, block_rows):
    columns_n, feat_total = w_qkv.shape
    wide = w_qkv.astype(jnp.float32)
    scaled = (wide * ln_gain[None, :]).astype(jnp.bfloat16)
    column_sum = jnp.sum(scaled.astype(jnp.float32), axis=1, keepdims=True)
    shift = jnp.sum(wide * ln_bias[None, :], axis=1) + b_qkv.astype(jnp.float32)
    ones = jnp.ones((SUMS, feat_total), jnp.bfloat16)
    weight = jnp.concatenate([scaled, ones], axis=0)
    share = feat_total // len(origins)
    inside = jnp.arange(share, dtype=jnp.int32)
    order = (jnp.stack(origins)[:, None] * share + inside[None, :]).reshape(-1)
    places = jnp.arange(feat_total, dtype=jnp.int32)
    moved = (places[:, None] == order[None, :]).astype(jnp.bfloat16)
    weight = jnp.dot(weight, moved, preferred_element_type=jnp.bfloat16)
    column_sum = jnp.broadcast_to(column_sum, (columns_n, block_rows))
    shift = jnp.broadcast_to(shift[:, None], (columns_n, block_rows))
    return weight, column_sum, shift


def encode(early, late, counts, weight, column_sum, shift):
    blocks_n, feat_share, block_rows = late[0].shape
    feat_total = weight.shape[1]
    cut = feat_share * len(early)
    rows_n = blocks_n * block_rows
    vmem = pl.BlockSpec(memory_space=pltpu.VMEM)
    params = pltpu.CompilerParams(vmem_limit_bytes=24 * 2**20)
    wide = jax.ShapeDtypeStruct(
        (blocks_n // GROUP, weight.shape[0], GROUP * block_rows), jnp.float32
    )
    before = pl.pallas_call(
        project_kernel,
        in_specs=[vmem] * (1 + len(early)),
        out_specs=vmem,
        out_shape=wide,
        compiler_params=params,
        cost_estimate=pl.CostEstimate(
            flops=2 * rows_n * weight.shape[0] * cut,
            bytes_accessed=rows_n * (2 * cut + 4 * weight.shape[0]),
            transcendentals=0,
        ),
    )(weight[:, :cut], *early)
    return pl.pallas_call(
        functools.partial(attend_kernel, feat_total),
        in_specs=[pl.BlockSpec(memory_space=pltpu.SMEM)] + [vmem] * (4 + len(late)),
        out_specs=vmem,
        out_shape=jax.ShapeDtypeStruct((blocks_n, feat_share, block_rows), jnp.bfloat16),
        compiler_params=params,
        cost_estimate=pl.CostEstimate(
            flops=2 * rows_n * weight.shape[0] * (feat_total - cut),
            bytes_accessed=rows_n * 4 * weight.shape[0],
            transcendentals=rows_n * block_rows,
        ),
    )(counts, weight[:, cut:], column_sum, shift, before, *late)


def rebalance(patches, counts, dest_ranks, dest_slots, ready):
    rank_total = lax.axis_size("dp")
    home_blocks = patches.shape[0]
    work_blocks = home_blocks // 2
    staying = dest_ranks == lax.axis_index("dp")
    positions = jnp.arange(home_blocks, dtype=jnp.int32)
    work_slots = jnp.arange(work_blocks, dtype=jnp.int32)
    filling = (dest_slots[None, :] == work_slots[:, None]) & (counts[None, :] > 0)

    def picked(which, values):
        return jnp.sum(jnp.where(filling & which[None, :], values[None, :], 0), axis=1)

    leaving_counts = picked(~staying, counts)
    staying_counts = picked(staying, counts)
    label_block = jnp.zeros((1,) + patches.shape[1:], patches.dtype)
    label_block = lax.dynamic_update_slice(
        label_block, leaving_counts.astype(patches.dtype)[None, None], (0, 0, 0)
    )
    message = jnp.concatenate([patches[picked(~staying, positions)], label_block], axis=0)
    pairs = [(source, (source + rank_total // 2) % rank_total) for source in range(rank_total)]
    arrived = lax.ppermute(message, "dp", pairs)
    sources = jnp.where(staying_counts > 0, picked(staying, positions), home_blocks + work_slots)
    arrived, sources, ready = lax.optimization_barrier((arrived, sources, ready))
    arrived_counts = arrived[work_blocks, 0, :work_blocks].astype(jnp.int32)
    pool = jnp.concatenate([patches, arrived], axis=0)
    work_counts = jnp.where(staying_counts > 0, staying_counts, arrived_counts)
    return pool[sources], work_counts, ready


def sense_of(rank):
    return 1 - 2 * (rank % 2)


def gather_pieces(own):
    rank_total, ring = lax.axis_size("dp"), lax.axis_size("fsdp")
    half = ring // 2

    swaps = [(rank, rank ^ 1) for rank in range(rank_total)]
    hops = [
        (rank * ring + place, rank * ring + (place + sense_of(rank)) % ring)
        for rank in range(rank_total)
        for place in range(ring)
    ]

    def swap(value):
        return lax.ppermute(value, "dp", swaps)

    def hop(value):
        return lax.ppermute(value, ("dp", "fsdp"), hops)

    mine, other, swapped = [own, hop(own)], [swap(own)], {}
    for step in range(1, half):
        received = hop(other[-1])
        other.append(received)
        mine[-1], other[-2] = lax.optimization_barrier((mine[-1], other[-2]))
        if step > 2:
            other[-1], swapped[step - 2] = lax.optimization_barrier((received, swapped[step - 2]))
        if step == half - 2:
            other[-1], swapped[step - 1] = lax.optimization_barrier((other[-1], swapped[step - 1]))
        mine.append(hop(mine[-1]))
        swapped[step] = swap(received)
    early = mine[:half] + [swapped[step] for step in range(1, half - 1)]
    return early, [mine[half], swapped[half - 1]]


def shards(patches, patch_count, dest_rank, dest_slot, ln_gain, ln_bias, w_qkv, b_qkv):
    ring = lax.axis_size("fsdp")
    half = ring // 2
    place = lax.axis_index("fsdp")
    sense = sense_of(lax.axis_index("dp"))
    origins = [(place - sense * step) % ring for step in range(half)]
    origins += [(place + sense * step) % ring for step in range(1, half - 1)]
    origins += [(place - sense * half) % ring, (place + sense * (half - 1)) % ring]
    weight, column_sum, shift = folded(
        ln_gain, ln_bias, w_qkv, b_qkv, origins, patches.shape[2]
    )
    own, counts, ready = rebalance(
        patches, patch_count[0], dest_rank[0], dest_slot[0], (weight, column_sum, shift)
    )
    return encode(*gather_pieces(own), counts, *ready)


def solution(mesh):
    placed = (
        P("dp", "fsdp", None),
        P("dp", None),
        P("dp", None),
        P("dp", None),
        P(),
        P(),
        P("fsdp", None),
        P("fsdp"),
    )
    return jax.shard_map(
        shards, mesh=mesh, in_specs=placed, out_specs=P("dp", "fsdp", None), check_vma=False
    )
```

```python
import functools
import math

import jax
import jax.numpy as jnp
from jax import lax
from jax.experimental import pallas as pl
from jax.experimental.pallas import tpu as pltpu
from jax.sharding import PartitionSpec as P

HEAD_DIM = 80
GROUP = 12
SUMS = 16


def project_group(weight, pieces, first):
    _, feat_share, block_rows = pieces[0].shape
    feat_total = feat_share * len(pieces)
    blocks, squares = [], []
    for block in range(GROUP):
        raw = jnp.concatenate([piece[first + block] for piece in pieces], axis=0)
        values = raw.astype(jnp.float32)
        squares.append(jnp.sum((values * values).reshape(feat_total // 8, 8, block_rows), axis=0))
        blocks.append(raw)
    product = jnp.dot(
        weight[...], jnp.concatenate(blocks, axis=1), preferred_element_type=jnp.float32
    )
    return product[:-8], jnp.concatenate(squares, axis=1)


def project_kernel(weight, *refs):
    pieces, out = refs[:-1], refs[-1]

    @pl.loop(0, out.shape[0])
    def _(index):
        product, squares = project_group(weight, pieces, index * GROUP)
        out[index, :-8] = product
        out[index, -8:] = squares


def attend_kernel(feat_total, counts, weight, column_sum, shift, before, *refs):
    pieces, out = refs[:-1], refs[-1]
    blocks_n, feat_share, block_rows = out.shape
    columns_n = column_sum.shape[0]
    key_place = lax.broadcasted_iota(jnp.int32, (block_rows, block_rows), 0)
    row_place = lax.broadcasted_iota(jnp.int32, (feat_share, block_rows), 1)

    @pl.loop(0, blocks_n // GROUP)
    def _(index):
        first = index * GROUP
        product, squares = project_group(weight, pieces, first)
        product = product + before[index, :-8]
        squares = jnp.sum(squares + before[index, -8:], axis=0, keepdims=True)
        center = product[columns_n : columns_n + 1] / feat_total
        spread = squares / feat_total - center * center
        scale = lax.rsqrt(spread + 1e-06)
        for block in range(GROUP):
            columns = slice(block * block_rows, (block + 1) * block_rows)
            part = (product[:columns_n, columns] - column_sum[...] * center[:, columns]) * scale[:, columns]
            qkv = (part + shift[...]).astype(jnp.bfloat16)
            count = counts[first + block]
            scores = lax.dot_general(
                qkv[HEAD_DIM : 2 * HEAD_DIM],
                qkv[:HEAD_DIM],
                (((0,), (0,)), ((), ())),
                preferred_element_type=jnp.float32,
            ) * (1.0 / math.sqrt(HEAD_DIM))
            raised = jnp.where(key_place < count, jnp.exp(scores), 0.0)
            totals = jnp.sum(raised, axis=0, keepdims=True)
            totals = jnp.where(count > 0, totals, 1.0)
            weights = (raised * (1.0 / totals)).astype(jnp.bfloat16)
            mixed = jnp.dot(qkv[2 * HEAD_DIM :], weights, preferred_element_type=jnp.float32)
            out[first + block] = jnp.where(row_place < count, mixed, 0.0).astype(jnp.bfloat16)


def folded(ln_gain, ln_bias, w_qkv, b_qkv, origins, block_rows):
    columns_n, feat_total = w_qkv.shape
    wide = w_qkv.astype(jnp.float32)
    scaled = (wide * ln_gain[None, :]).astype(jnp.bfloat16)
    column_sum = jnp.sum(scaled.astype(jnp.float32), axis=1, keepdims=True)
    shift = jnp.sum(wide * ln_bias[None, :], axis=1) + b_qkv.astype(jnp.float32)
    ones = jnp.ones((SUMS, feat_total), jnp.bfloat16)
    weight = jnp.concatenate([scaled, ones], axis=0)
    share = feat_total // len(origins)
    inside = jnp.arange(share, dtype=jnp.int32)
    order = (jnp.stack(origins)[:, None] * share + inside[None, :]).reshape(-1)
    places = jnp.arange(feat_total, dtype=jnp.int32)
    moved = (places[:, None] == order[None, :]).astype(jnp.bfloat16)
    weight = jnp.dot(weight, moved, preferred_element_type=jnp.bfloat16)
    column_sum = jnp.broadcast_to(column_sum, (columns_n, block_rows))
    shift = jnp.broadcast_to(shift[:, None], (columns_n, block_rows))
    return weight, column_sum, shift


def encode(early, late, counts, weight, column_sum, shift):
    blocks_n, feat_share, block_rows = late[0].shape
    feat_total = weight.shape[1]
    cut = feat_share * len(early)
    rows_n = blocks_n * block_rows
    vmem = pl.BlockSpec(memory_space=pltpu.VMEM)
    params = pltpu.CompilerParams(vmem_limit_bytes=24 * 2**20)
    wide = jax.ShapeDtypeStruct(
        (blocks_n // GROUP, weight.shape[0], GROUP * block_rows), jnp.float32
    )
    before = pl.pallas_call(
        project_kernel,
        in_specs=[vmem] * (1 + len(early)),
        out_specs=vmem,
        out_shape=wide,
        compiler_params=params,
        cost_estimate=pl.CostEstimate(
            flops=2 * rows_n * weight.shape[0] * cut,
            bytes_accessed=rows_n * (2 * cut + 4 * weight.shape[0]),
            transcendentals=0,
        ),
    )(weight[:, :cut], *early)
    return pl.pallas_call(
        functools.partial(attend_kernel, feat_total),
        in_specs=[pl.BlockSpec(memory_space=pltpu.SMEM)] + [vmem] * (4 + len(late)),
        out_specs=vmem,
        out_shape=jax.ShapeDtypeStruct((blocks_n, feat_share, block_rows), jnp.bfloat16),
        compiler_params=params,
        cost_estimate=pl.CostEstimate(
            flops=2 * rows_n * weight.shape[0] * (feat_total - cut),
            bytes_accessed=rows_n * 4 * weight.shape[0],
            transcendentals=rows_n * block_rows,
        ),
    )(counts, weight[:, cut:], column_sum, shift, before, *late)


def rebalance(patches, counts, dest_ranks, dest_slots, ready):
    rank_total = lax.axis_size("dp")
    home_blocks = patches.shape[0]
    work_blocks = home_blocks // 2
    staying = dest_ranks == lax.axis_index("dp")
    positions = jnp.arange(home_blocks, dtype=jnp.int32)
    work_slots = jnp.arange(work_blocks, dtype=jnp.int32)
    filling = (dest_slots[None, :] == work_slots[:, None]) & (counts[None, :] > 0)

    def picked(which, values):
        return jnp.sum(jnp.where(filling & which[None, :], values[None, :], 0), axis=1)

    leaving_counts = picked(~staying, counts)
    staying_counts = picked(staying, counts)
    label_block = jnp.zeros((1,) + patches.shape[1:], patches.dtype)
    label_block = lax.dynamic_update_slice(
        label_block, leaving_counts.astype(patches.dtype)[None, None], (0, 0, 0)
    )
    message = jnp.concatenate([patches[picked(~staying, positions)], label_block], axis=0)
    pairs = [(source, (source + rank_total // 2) % rank_total) for source in range(rank_total)]
    arrived = lax.ppermute(message, "dp", pairs)
    sources = jnp.where(staying_counts > 0, picked(staying, positions), home_blocks + work_slots)
    arrived, sources, ready = lax.optimization_barrier((arrived, sources, ready))
    arrived_counts = arrived[work_blocks, 0, :work_blocks].astype(jnp.int32)
    pool = jnp.concatenate([patches, arrived], axis=0)
    work_counts = jnp.where(staying_counts > 0, staying_counts, arrived_counts)
    return pool[sources], work_counts, ready


def sense_of(rank):
    return 1 - 2 * (rank % 2)


def gather_pieces(own):
    rank_total, ring = lax.axis_size("dp"), lax.axis_size("fsdp")
    half = ring // 2

    swaps = [(rank, rank ^ 1) for rank in range(rank_total)]
    hops = [
        (rank * ring + place, rank * ring + (place + sense_of(rank)) % ring)
        for rank in range(rank_total)
        for place in range(ring)
    ]

    def swap(value):
        return lax.ppermute(value, "dp", swaps)

    def hop(value):
        return lax.ppermute(value, ("dp", "fsdp"), hops)

    mine, other, swapped = [own, hop(own)], [swap(own)], {}
    for step in range(1, half):
        received = hop(other[-1])
        other.append(received)
        mine[-1], other[-2] = lax.optimization_barrier((mine[-1], other[-2]))
        if step > 2:
            other[-1], swapped[step - 2] = lax.optimization_barrier((received, swapped[step - 2]))
        if step == half - 2:
            other[-1], swapped[step - 1] = lax.optimization_barrier((other[-1], swapped[step - 1]))
        mine.append(hop(mine[-1]))
        if step != half - 2:
            swapped[step] = swap(received)
    before_last = lax.optimization_barrier((other[half - 2], other[half - 1]))[0]
    swapped[half - 2] = swap(before_last)
    early = mine[:half] + [swapped[step] for step in range(1, half - 2)]
    return early, [mine[half], swapped[half - 2], swapped[half - 1]]


def shards(patches, patch_count, dest_rank, dest_slot, ln_gain, ln_bias, w_qkv, b_qkv):
    ring = lax.axis_size("fsdp")
    half = ring // 2
    place = lax.axis_index("fsdp")
    sense = sense_of(lax.axis_index("dp"))
    origins = [(place - sense * step) % ring for step in range(half)]
    origins += [(place + sense * step) % ring for step in range(1, half - 2)]
    origins += [(place - sense * half) % ring]
    origins += [(place + sense * step) % ring for step in range(half - 2, half)]
    weight, column_sum, shift = folded(
        ln_gain, ln_bias, w_qkv, b_qkv, origins, patches.shape[2]
    )
    own, counts, ready = rebalance(
        patches, patch_count[0], dest_rank[0], dest_slot[0], (weight, column_sum, shift)
    )
    return encode(*gather_pieces(own), counts, *ready)


def solution(mesh):
    placed = (
        P("dp", "fsdp", None),
        P("dp", None),
        P("dp", None),
        P("dp", None),
        P(),
        P(),
        P("fsdp", None),
        P("fsdp"),
    )
    return jax.shard_map(
        shards, mesh=mesh, in_specs=placed, out_specs=P("dp", "fsdp", None), check_vma=False
    )
```
